32 devices in a mesh: tm: 8 (over y, x, core), sta: 4 (over z).
Axes of the slice: x: 2, y: 2, z: 4, core: 2. Of those that a mesh axis runs over, the one named last changes fastest.
Arguments:
- spectra: bfloat16 [16, 128, 6, 1024], P('tm', 'sta'), may hold values from -6 to 6
- pairs: int32 [4, 4, 2, 16], P('sta'), may hold values from 0 to 31
- counts: int32 [4, 4], P('sta'), may hold values from 3 to 16, as said below
Outputs:
- correlations: bfloat16 [4, 4, 16, 9, 4001], P('sta', None, 'tm')
The draws below stay inside these ranges and needn't reach their ends.
Inputs may be any that keep to these rules, and one draw needn't show every extreme that they name: `counts`: pair slots at or after a tile's count are ignored; the tiles of shift 0 use all 16 slots.
All inputs are finite; a program needn't handle non-finite values.
Results may differ from the reference program's by a relative error of at most 0.014.
Values may be sent and summed in bfloat16 or wider, within the bound.
A program may use at most 64 MiB of HBM per device.

```python
import math
import jax
import jax.numpy as jnp
from jax import lax

NF = 1024
NFFT = 8192
LAGS = 4001
BAND = 64
SB = 32
HD = 2
P_TILE = 16
HOURS = 16
STATIONS = 128
N_TM = 8
N_STA = 4


def draw_counts(key, part):
    drawn = jax.random.randint(key, (N_STA, N_STA), P_TILE // 5, P_TILE + 1, dtype=jnp.int32)
    return drawn.at[:, 0].set(P_TILE)


def plant(array, key, least, largest):
    spot = [jax.random.randint(jax.random.fold_in(key, axis), (), 0, length) for axis, length in enumerate(array.shape)]
    widest = array.shape.index(max(array.shape))
    next_to = spot[:widest] + [(spot[widest] + 1) % array.shape[widest]] + spot[widest + 1:]
    return array.at[tuple(spot)].set(least).at[tuple(next_to)].set(largest)


def block_scale(key, extent, cuts, low, largest):
    level, own = 1.0, jax.random.fold_in(key, 6)
    for dim, blocks in cuts:
        steps = jnp.exp(jax.random.uniform(jax.random.fold_in(own, dim), (blocks,), jnp.float32, low / len(cuts), largest / len(cuts)))
        level = level * jnp.repeat(steps, extent[dim] // blocks).reshape([-1 if axis == dim else 1 for axis in range(len(extent))])
    return level


def scatter_about(key, dims, spread, limit, shards=(), held_as=jnp.bfloat16):
    loudness = block_scale(key, dims, shards, -0.22, 0.18) if shards else 1.0
    values = jax.random.normal(key, dims, jnp.float32) * spread * loudness
    return jnp.minimum(jnp.maximum(values, -limit), limit).astype(held_as)


def setup_inputs(seed: int = 0) -> dict:
    arg_keys = jax.random.split(jax.random.key(seed), 4)
    return {
        "spectra": scatter_about(arg_keys[0], (HOURS, STATIONS, 6, NF), 1.0, 6.0, ((0, 8), (1, 4))),
        "pairs": plant(jax.random.randint(arg_keys[1], (N_STA, N_STA, 2, P_TILE), 0, SB), jax.random.fold_in(arg_keys[1], 1), 0, SB - 1).astype(jnp.int32),
        "counts": draw_counts(jax.random.fold_in(arg_keys[3], 71), 0),
    }


def whiten(spectra):
    lead = spectra.shape[:-2]
    values = spectra.astype(jnp.float32).reshape(lead + (3, 2, NF // BAND, BAND))
    power = lax.optimization_barrier(jnp.mean(values[..., 0, :, :] ** 2 + values[..., 1, :, :] ** 2, axis=-1))
    scaled = values * lax.rsqrt(power[..., None, :, None] + 1e-06)
    return scaled.reshape(lead + (6, NF)).astype(jnp.bfloat16)

def cross(own_rows, visit_rows):
    hours_n, slots = (own_rows.shape[0], own_rows.shape[1])
    first = own_rows.astype(jnp.float32).reshape(hours_n, slots, 3, 2, NF)
    second = visit_rows.astype(jnp.float32).reshape(hours_n, slots, 3, 2, NF)
    are, aim = (first[:, :, :, 0][:, :, :, None], first[:, :, :, 1][:, :, :, None])
    bre, bim = (second[:, :, :, 0][:, :, None], second[:, :, :, 1][:, :, None])
    real_part = lax.optimization_barrier(jnp.sum(are * bre + aim * bim, axis=0)).reshape(slots, 9, NF)
    imag_part = lax.optimization_barrier(jnp.sum(are * bim - aim * bre, axis=0)).reshape(slots, 9, NF)
    return jnp.concatenate([real_part, imag_part], axis=-1)

def make_table():
    freqs = jnp.arange(NF, dtype=jnp.int32)
    shifts = jnp.arange(LAGS, dtype=jnp.int32) - (LAGS - 1) // 2
    phase = jnp.mod(freqs[:, None] * shifts[None, :], NFFT)
    angle = 2.0 * math.pi / NFFT * phase.astype(jnp.float32)
    return jnp.concatenate([jnp.cos(angle), -jnp.sin(angle)], axis=0).astype(jnp.bfloat16)

def reference(spectra, pairs, counts):
    white = whiten(spectra).reshape(N_TM, HD, N_STA, SB, 6, NF)
    table = make_table().astype(jnp.float32)
    scale = 1.0 / math.sqrt(HOURS * NF)

    def one_tile(index):
        blk = index // N_STA
        shift = index % N_STA
        other = jnp.mod(blk - shift, N_STA)
        own = lax.dynamic_index_in_dim(white, blk, 2, keepdims=False)
        visit = lax.dynamic_index_in_dim(white, other, 2, keepdims=False)
        first_idx = pairs[blk, shift, 0]
        second_idx = pairs[blk, shift, 1]
        keep = (jnp.arange(P_TILE, dtype=jnp.int32) < counts[blk, shift]).astype(jnp.float32)

        def per_device(carry, item):
            own_t, visit_t = item
            term = cross(jnp.take(own_t, first_idx, axis=1), jnp.take(visit_t, second_idx, axis=1))
            term = term * keep[:, None, None]
            rounded = lax.optimization_barrier(term.astype(jnp.bfloat16)).astype(jnp.float32)
            return (carry + rounded, None)
        total, _ = lax.scan(per_device, jnp.zeros((P_TILE, 9, 2 * NF), jnp.float32), (own, visit))
        spectrum = total.astype(jnp.bfloat16).astype(jnp.float32).reshape(P_TILE * 9, 2 * NF)
        lagged = jnp.dot(spectrum, table, preferred_element_type=jnp.float32) * scale
        return lagged.astype(jnp.bfloat16).reshape(P_TILE, 9, LAGS)
    tiles = lax.map(one_tile, jnp.arange(N_STA * N_STA, dtype=jnp.int32))
    return tiles.reshape(N_STA, N_STA, P_TILE, 9, LAGS)
```

```python
import math

import jax
import jax.numpy as jnp
import ml_dtypes
import numpy as np
from jax import lax
from jax.sharding import PartitionSpec as P

NF = 1024
NFFT = 8192
LAGS = 4001
BAND = 64


def shifted(value, axis, steps):
    count = lax.axis_size(axis)
    pairs = [(source, (source + steps) % count) for source in range(count)]
    return lax.ppermute(value, axis, pairs)


def make_table():
    freqs = np.arange(NF, dtype=np.int64)
    shifts = np.arange(LAGS, dtype=np.int64) - (LAGS - 1) // 2
    phase = np.mod(freqs[:, None] * shifts[None, :], NFFT)
    steps = np.arange(NFFT, dtype=np.float64) * (2.0 * math.pi / NFFT)
    cosine = np.cos(steps).astype(np.float32).astype(ml_dtypes.bfloat16)
    sine = (-np.sin(steps)).astype(np.float32).astype(ml_dtypes.bfloat16)
    return np.concatenate([cosine[phase], sine[phase]], axis=0)


def whiten(spectra):
    lead = spectra.shape[:-2]
    values = spectra.astype(jnp.float32).reshape(lead + (3, 2, NF // BAND, BAND))
    power = jnp.mean(values[..., 0, :, :] ** 2 + values[..., 1, :, :] ** 2, axis=-1)
    scaled = values * lax.rsqrt(power[..., None, :, None] + 1e-06)
    return scaled.reshape(lead + (6, NF)).astype(jnp.bfloat16)


def pick(white, idx):
    hot = (idx[:, None] == jnp.arange(white.shape[1], dtype=jnp.int32)[None, :]).astype(jnp.bfloat16)
    flat = white.reshape(white.shape[0], white.shape[1], -1)
    hot = jnp.broadcast_to(hot[None], (white.shape[0],) + hot.shape)
    out = jnp.einsum("hps,hsx->hpx", hot, flat, preferred_element_type=jnp.float32)
    return out.astype(jnp.bfloat16).reshape(white.shape[0], idx.shape[0], 6, -1)


def cross(own_rows, visit_rows):
    hours_n, slots, bins = (own_rows.shape[0], own_rows.shape[1], own_rows.shape[-1])
    first = own_rows.astype(jnp.float32).reshape(hours_n, slots, 3, 2, bins)
    second = visit_rows.astype(jnp.float32).reshape(hours_n, slots, 3, 2, bins)
    are, aim = (first[:, :, :, 0][:, :, :, None], first[:, :, :, 1][:, :, :, None])
    bre, bim = (second[:, :, :, 0][:, :, None], second[:, :, :, 1][:, :, None])
    real_part = jnp.sum(are * bre + aim * bim, axis=0).reshape(slots, 9, bins)
    imag_part = jnp.sum(are * bim - aim * bre, axis=0).reshape(slots, 9, bins)
    return jnp.concatenate([real_part, imag_part], axis=-1)


def per_device(table, spectra, pairs, counts):
    n_tm = lax.axis_size("tm")
    n_sta = lax.axis_size("sta")
    hours_dev = spectra.shape[0]
    p_tile = pairs.shape[3]
    owned = p_tile // n_tm
    asked = [pairs[0, 0, 1]] + [
        shifted(pairs[0, step, 1], "sta", -step) for step in range(1, n_sta)
    ]
    white = whiten(spectra)
    visits = [pick(white, asked[0])] + [
        shifted(pick(white, asked[step]), "sta", step) for step in range(1, n_sta)
    ]

    def reduce_tile(shift):
        limit = counts[0, shift]
        value = cross(pick(white, pairs[0, shift, 0]), visits[shift])
        slots = jnp.arange(p_tile, dtype=jnp.int32)
        value = jnp.where((slots < limit)[:, None, None], value, 0.0)
        return lax.psum_scatter(
            value.astype(jnp.bfloat16), "tm", scatter_dimension=0, tiled=True
        )

    reduced = [reduce_tile(shift) for shift in range(n_sta)]
    rows = jnp.stack(reduced, axis=0).reshape(n_sta * owned * 9, 2 * NF)
    lagged = jnp.dot(rows, table, preferred_element_type=jnp.float32)
    scale = 1.0 / math.sqrt(hours_dev * n_tm * NF)
    return (lagged * scale).astype(jnp.bfloat16).reshape(1, n_sta, owned, 9, LAGS)


def solution(mesh):
    mapped = jax.shard_map(
        per_device,
        mesh=mesh,
        in_specs=(
            P(None, None),
            P("tm", "sta", None, None),
            P("sta", None, None, None),
            P("sta", None),
        ),
        out_specs=P("sta", None, "tm", None, None),
        check_vma=False,
    )
    table = make_table()

    def run(spectra, pairs, counts):
        return mapped(jnp.asarray(table), spectra, pairs, counts)

    return run
```

```python
import math

import jax
import jax.numpy as jnp
import ml_dtypes
import numpy as np
from jax import lax
from jax.sharding import PartitionSpec as P

NF = 1024
NFFT = 8192
LAGS = 4001
BAND = 64


def shifted(value, axis, steps):
    count = lax.axis_size(axis)
    pairs = [(source, (source + steps) % count) for source in range(count)]
    return lax.ppermute(value, axis, pairs)


def make_table():
    freqs = np.arange(NF, dtype=np.int64)
    shifts = np.arange(LAGS, dtype=np.int64) - (LAGS - 1) // 2
    phase = np.mod(freqs[:, None] * shifts[None, :], NFFT)
    steps = np.arange(NFFT, dtype=np.float64) * (2.0 * math.pi / NFFT)
    cosine = np.cos(steps).astype(np.float32).astype(ml_dtypes.bfloat16)
    sine = (-np.sin(steps)).astype(np.float32).astype(ml_dtypes.bfloat16)
    return np.concatenate([cosine[phase], sine[phase]], axis=0)


def whiten(spectra):
    lead = spectra.shape[:-2]
    values = spectra.astype(jnp.float32).reshape(lead + (3, 2, NF // BAND, BAND))
    power = jnp.mean(values[..., 0, :, :] ** 2 + values[..., 1, :, :] ** 2, axis=-1)
    scaled = values * lax.rsqrt(power[..., None, :, None] + 1e-06)
    return scaled.reshape(lead + (6, NF)).astype(jnp.bfloat16)


def pick(white, idx):
    hot = (idx[:, None] == jnp.arange(white.shape[1], dtype=jnp.int32)[None, :]).astype(jnp.bfloat16)
    flat = white.reshape(white.shape[0], white.shape[1], -1)
    hot = jnp.broadcast_to(hot[None], (white.shape[0],) + hot.shape)
    out = jnp.einsum("hps,hsx->hpx", hot, flat, preferred_element_type=jnp.float32)
    return out.astype(jnp.bfloat16).reshape(white.shape[0], idx.shape[0], 6, -1)


def cross(own_rows, visit_rows):
    hours_n, slots, bins = (own_rows.shape[0], own_rows.shape[1], own_rows.shape[-1])
    first = own_rows.astype(jnp.float32).reshape(hours_n, slots, 3, 2, bins // 128, 128)
    second = visit_rows.astype(jnp.float32).reshape(hours_n, slots, 3, 2, bins // 128, 128)
    are, aim = (first[:, :, :, 0][:, :, :, None], first[:, :, :, 1][:, :, :, None])
    bre, bim = (second[:, :, :, 0][:, :, None], second[:, :, :, 1][:, :, None])
    real_part = jnp.sum(are * bre + aim * bim, axis=0).reshape(slots, 9, bins // 128, 128)
    imag_part = jnp.sum(are * bim - aim * bre, axis=0).reshape(slots, 9, bins // 128, 128)
    return jnp.concatenate([real_part, imag_part], axis=-2)


def sum_at_owner(value, axis, turn):
    count = lax.axis_size(axis)
    if count & (count - 1):
        return lax.psum_scatter(value, axis, scatter_dimension=0, tiled=True)
    owned, tail = value.shape[0] // count, value.shape[1:]
    bits = list(range(count.bit_length() - 1))
    others = bits[1:]
    if others:
        cut = turn % len(others)
        bits = bits[:1] + others[cut:] + others[:cut]
    me = lax.axis_index(axis)
    left = count.bit_length() - 1
    value = value.reshape((2,) * left + (owned,) + tail)
    for bit in bits:
        mine = lax.rem(lax.div(me, jnp.int32(1 << bit)), jnp.int32(2))
        dim = left - 1 - bit
        keep = lax.dynamic_slice_in_dim(value, mine, 1, dim)
        give = lax.dynamic_slice_in_dim(value, 1 - mine, 1, dim)
        swap = [(source, source ^ (1 << bit)) for source in range(count)]
        got = lax.ppermute(give.astype(jnp.bfloat16), axis, swap)
        value = keep.astype(jnp.float32) + got.astype(jnp.float32)
    return value.reshape((owned,) + tail)


def per_device(table, spectra, pairs, counts):
    n_tm = lax.axis_size("tm")
    n_sta = lax.axis_size("sta")
    hours_dev = spectra.shape[0]
    p_tile = pairs.shape[3]
    owned = p_tile // n_tm
    asked = [pairs[0, 0, 1]] + [
        shifted(pairs[0, step, 1], "sta", -step) for step in range(1, n_sta)
    ]
    white = whiten(spectra)
    visits = [pick(white, asked[0])] + [
        shifted(pick(white, asked[step]), "sta", step) for step in range(1, n_sta)
    ]

    def reduce_tile(shift):
        limit = counts[0, shift]
        value = cross(pick(white, pairs[0, shift, 0]), visits[shift])
        slots = jnp.arange(p_tile, dtype=jnp.int32)
        value = jnp.where((slots < limit)[:, None, None, None], value, 0.0)
        return sum_at_owner(value.astype(jnp.bfloat16), "tm", shift)

    reduced = [reduce_tile(shift) for shift in range(n_sta)]
    rows = jnp.stack(reduced, axis=0).astype(jnp.bfloat16).reshape(n_sta * owned * 9, 2 * NF)
    lagged = jnp.dot(rows, table, preferred_element_type=jnp.float32)
    scale = 1.0 / math.sqrt(hours_dev * n_tm * NF)
    return (lagged * scale).astype(jnp.bfloat16).reshape(1, n_sta, owned, 9, LAGS)


def solution(mesh):
    mapped = jax.shard_map(
        per_device,
        mesh=mesh,
        in_specs=(
            P(None, None),
            P("tm", "sta", None, None),
            P("sta", None, None, None),
            P("sta", None),
        ),
        out_specs=P("sta", None, "tm", None, None),
        check_vma=False,
    )
    table = make_table()

    def run(spectra, pairs, counts):
        return mapped(jnp.asarray(table), spectra, pairs, counts)

    return run
```

```python
import math

import jax
import jax.numpy as jnp
import ml_dtypes
import numpy as np
from jax import lax
from jax.sharding import PartitionSpec as P

NF = 1024
NFFT = 8192
LAGS = 4001
BAND = 64


def shifted(value, axis, steps):
    count = lax.axis_size(axis)
    pairs = [(source, (source + steps) % count) for source in range(count)]
    return lax.ppermute(value, axis, pairs)


def make_table():
    freqs = np.arange(NF, dtype=np.int64)
    shifts = np.arange(LAGS, dtype=np.int64) - (LAGS - 1) // 2
    phase = np.mod(freqs[:, None] * shifts[None, :], NFFT)
    steps = np.arange(NFFT, dtype=np.float64) * (2.0 * math.pi / NFFT)
    cosine = np.cos(steps).astype(np.float32).astype(ml_dtypes.bfloat16)
    sine = (-np.sin(steps)).astype(np.float32).astype(ml_dtypes.bfloat16)
    return np.concatenate([cosine[phase], sine[phase]], axis=0)


def whiten(spectra):
    lanes = spectra.shape[-1]
    per_row = lanes // BAND
    values = spectra.astype(jnp.float32).reshape(spectra.shape[:2] + (3, 2) + spectra.shape[3:])
    square = values[:, :, :, 0] ** 2 + values[:, :, :, 1] ** 2
    band = jnp.arange(lanes, dtype=jnp.int32) // BAND
    inverse = jnp.zeros_like(square)
    for index in range(per_row):
        inside = band == index
        power = jnp.sum(jnp.where(inside, square, 0.0), axis=-1, keepdims=True) * (1.0 / BAND)
        inverse = jnp.where(inside, lax.rsqrt(power + 1e-06), inverse)
    return (values * inverse[:, :, :, None]).astype(jnp.bfloat16)


def pick(white, idx):
    hot = (idx[:, None] == jnp.arange(white.shape[1], dtype=jnp.int32)[None, :]).astype(jnp.bfloat16)
    flat = white.reshape(white.shape[0], white.shape[1], -1)
    hot = jnp.broadcast_to(hot[None], (white.shape[0],) + hot.shape)
    out = jnp.einsum("hps,hsx->hpx", hot, flat, preferred_element_type=jnp.float32)
    return out.astype(jnp.bfloat16).reshape(white.shape[0], idx.shape[0], 6, -1, 128)


def cross(own_rows, visit_rows):
    slots, tiles = (own_rows.shape[1], own_rows.shape[-2:])
    first, second = (own_rows.astype(jnp.float32), visit_rows.astype(jnp.float32))
    are, aim = (first[:, :, :, 0][:, :, :, None], first[:, :, :, 1][:, :, :, None])
    bre, bim = (second[:, :, :, 0][:, :, None], second[:, :, :, 1][:, :, None])
    real_part = jnp.sum(are * bre + aim * bim, axis=0).reshape((slots, 9) + tiles)
    imag_part = jnp.sum(are * bim - aim * bre, axis=0).reshape((slots, 9) + tiles)
    return jnp.concatenate([real_part, imag_part], axis=-2)


def sum_at_owner(value, axis, turn):
    count = lax.axis_size(axis)
    if count & (count - 1):
        return lax.psum_scatter(value, axis, scatter_dimension=0, tiled=True)
    owned, tail = value.shape[0] // count, value.shape[1:]
    bits = list(range(count.bit_length() - 1))
    others = bits[1:]
    if others:
        cut = turn % len(others)
        bits = bits[:1] + others[cut:] + others[:cut]
    me = lax.axis_index(axis)
    left = count.bit_length() - 1
    value = value.reshape((2,) * left + (owned,) + tail)
    for bit in bits:
        mine = lax.rem(lax.div(me, jnp.int32(1 << bit)), jnp.int32(2))
        dim = left - 1 - bit
        keep = lax.dynamic_slice_in_dim(value, mine, 1, dim)
        give = lax.dynamic_slice_in_dim(value, 1 - mine, 1, dim)
        swap = [(source, source ^ (1 << bit)) for source in range(count)]
        got = lax.ppermute(give.astype(jnp.bfloat16), axis, swap)
        value = keep.astype(jnp.float32) + got.astype(jnp.float32)
    return value.reshape((owned,) + tail)


def per_device(table, spectra, pairs, counts):
    n_tm = lax.axis_size("tm")
    n_sta = lax.axis_size("sta")
    hours_dev = spectra.shape[0]
    p_tile = pairs.shape[3]
    owned = p_tile // n_tm
    asked = [pairs[0, 0, 1]] + [
        shifted(pairs[0, step, 1], "sta", -step) for step in range(1, n_sta)
    ]
    visits = [pick(spectra, asked[0])] + [
        shifted(pick(spectra, asked[step]), "sta", step) for step in range(1, n_sta)
    ]

    def reduce_tile(shift):
        limit = counts[0, shift]
        value = cross(whiten(pick(spectra, pairs[0, shift, 0])), whiten(visits[shift]))
        slots = jnp.arange(p_tile, dtype=jnp.int32)
        value = jnp.where((slots < limit)[:, None, None, None], value, 0.0)
        return sum_at_owner(value.astype(jnp.bfloat16), "tm", shift)

    reduced = [reduce_tile(shift) for shift in range(n_sta)]
    rows = jnp.stack(reduced, axis=0).astype(jnp.bfloat16).reshape(n_sta * owned * 9, 2 * NF)
    lagged = jnp.dot(rows, table, preferred_element_type=jnp.float32)
    scale = 1.0 / math.sqrt(hours_dev * n_tm * NF)
    return (lagged * scale).astype(jnp.bfloat16).reshape(1, n_sta, owned, 9, LAGS)


def solution(mesh):
    mapped = jax.shard_map(
        per_device,
        mesh=mesh,
        in_specs=(
            P(None, None),
            P("tm", "sta", None, None),
            P("sta", None, None, None),
            P("sta", None),
        ),
        out_specs=P("sta", None, "tm", None, None),
        check_vma=False,
    )
    table = make_table()

    def run(spectra, pairs, counts):
        return mapped(jnp.asarray(table), spectra, pairs, counts)

    return run
```

```python
import math

import jax
import jax.numpy as jnp
import ml_dtypes
import numpy as np
from jax import lax
from jax.sharding import PartitionSpec as P

NF = 1024
NFFT = 8192
LAGS = 4001
BAND = 64


def shifted(value, axis, steps):
    count = lax.axis_size(axis)
    pairs = [(source, (source + steps) % count) for source in range(count)]
    return lax.ppermute(value, axis, pairs)


def make_table():
    freqs = np.arange(NF, dtype=np.int64)
    shifts = np.arange(LAGS, dtype=np.int64) - (LAGS - 1) // 2
    phase = np.mod(freqs[:, None] * shifts[None, :], NFFT)
    steps = np.arange(NFFT, dtype=np.float64) * (2.0 * math.pi / NFFT)
    cosine = np.cos(steps).astype(np.float32).astype(ml_dtypes.bfloat16)
    sine = (-np.sin(steps)).astype(np.float32).astype(ml_dtypes.bfloat16)
    return np.concatenate([cosine[phase], sine[phase]], axis=0)


def whiten(spectra):
    lanes = spectra.shape[-1]
    values = spectra.astype(jnp.float32).reshape(spectra.shape[:2] + (3, 2) + spectra.shape[3:])
    square = values[:, :, :, 0] ** 2 + values[:, :, :, 1] ** 2
    band = np.arange(lanes) // BAND
    mean = jnp.asarray((band[:, None] == band[None, :]).astype(np.float32) / BAND)
    power = jnp.dot(square, mean, precision=lax.Precision.HIGHEST, preferred_element_type=jnp.float32)
    inverse = lax.rsqrt(power + 1e-06)
    return (values * inverse[:, :, :, None]).astype(jnp.bfloat16)


def pick(white, idx):
    hot = (idx[:, None] == jnp.arange(white.shape[1], dtype=jnp.int32)[None, :]).astype(jnp.bfloat16)
    flat = white.reshape(white.shape[0], white.shape[1], -1)
    hot = jnp.broadcast_to(hot[None], (white.shape[0],) + hot.shape)
    out = jnp.einsum("hps,hsx->hpx", hot, flat, preferred_element_type=jnp.float32)
    return out.astype(jnp.bfloat16).reshape(white.shape[0], idx.shape[0], 6, -1, 128)


def cross(own_rows, visit_rows):
    slots, tiles = (own_rows.shape[1], own_rows.shape[-2:])
    first, second = (own_rows.astype(jnp.float32), visit_rows.astype(jnp.float32))
    are, aim = (first[:, :, :, 0][:, :, :, None], first[:, :, :, 1][:, :, :, None])
    bre, bim = (second[:, :, :, 0][:, :, None], second[:, :, :, 1][:, :, None])
    real_part = jnp.sum(are * bre + aim * bim, axis=0).reshape((slots, 9) + tiles)
    imag_part = jnp.sum(are * bim - aim * bre, axis=0).reshape((slots, 9) + tiles)
    return jnp.concatenate([real_part, imag_part], axis=-2)


def sum_at_owner(value, axis, turn):
    count = lax.axis_size(axis)
    if count & (count - 1):
        return lax.psum_scatter(value, axis, scatter_dimension=0, tiled=True)
    owned, tail = value.shape[0] // count, value.shape[1:]
    bits = list(range(count.bit_length() - 1))
    others = bits[1:]
    if others:
        cut = turn % len(others)
        bits = bits[:1] + others[cut:] + others[:cut]
    me = lax.axis_index(axis)
    left = count.bit_length() - 1
    value = value.reshape((2,) * left + (owned,) + tail)
    for bit in bits:
        mine = lax.rem(lax.div(me, jnp.int32(1 << bit)), jnp.int32(2))
        dim = left - 1 - bit
        keep = lax.dynamic_slice_in_dim(value, mine, 1, dim)
        give = lax.dynamic_slice_in_dim(value, 1 - mine, 1, dim)
        swap = [(source, source ^ (1 << bit)) for source in range(count)]
        got = lax.ppermute(give.astype(jnp.bfloat16), axis, swap)
        value = keep.astype(jnp.float32) + got.astype(jnp.float32)
    return value.reshape((owned,) + tail)


def per_device(table, spectra, pairs, counts):
    n_tm = lax.axis_size("tm")
    n_sta = lax.axis_size("sta")
    hours_dev = spectra.shape[0]
    p_tile = pairs.shape[3]
    owned = p_tile // n_tm
    asked = [pairs[0, 0, 1]] + [
        shifted(pairs[0, step, 1], "sta", -step) for step in range(1, n_sta)
    ]
    visits = [pick(spectra, asked[0])] + [
        shifted(pick(spectra, asked[step]), "sta", step) for step in range(1, n_sta)
    ]

    def reduce_tile(shift):
        limit = counts[0, shift]
        value = cross(whiten(pick(spectra, pairs[0, shift, 0])), whiten(visits[shift]))
        slots = jnp.arange(p_tile, dtype=jnp.int32)
        value = jnp.where((slots < limit)[:, None, None, None], value, 0.0)
        return sum_at_owner(value.astype(jnp.bfloat16), "tm", shift)

    reduced = [reduce_tile(shift) for shift in range(n_sta)]
    rows = jnp.stack(reduced, axis=0).astype(jnp.bfloat16).reshape(n_sta * owned * 9, 2 * NF)
    lagged = jnp.dot(rows, table, preferred_element_type=jnp.float32)
    scale = 1.0 / math.sqrt(hours_dev * n_tm * NF)
    return (lagged * scale).astype(jnp.bfloat16).reshape(1, n_sta, owned, 9, LAGS)


def solution(mesh):
    mapped = jax.shard_map(
        per_device,
        mesh=mesh,
        in_specs=(
            P(None, None),
            P("tm", "sta", None, None),
            P("sta", None, None, None),
            P("sta", None),
        ),
        out_specs=P("sta", None, "tm", None, None),
        check_vma=False,
    )
    table = make_table()

    def run(spectra, pairs, counts):
        return mapped(jnp.asarray(table), spectra, pairs, counts)

    return run
```

```python
import math

import jax
import jax.numpy as jnp
import ml_dtypes
import numpy as np
from jax import lax
from jax.sharding import PartitionSpec as P

NF = 1024
NFFT = 8192
LAGS = 4001
BAND = 64


def shifted(value, axis, steps):
    count = lax.axis_size(axis)
    pairs = [(source, (source + steps) % count) for source in range(count)]
    return lax.ppermute(value, axis, pairs)


def make_table():
    freqs = np.arange(NF, dtype=np.int64)
    shifts = np.arange(LAGS, dtype=np.int64) - (LAGS - 1) // 2
    phase = np.mod(freqs[:, None] * shifts[None, :], NFFT)
    steps = np.arange(NFFT, dtype=np.float64) * (2.0 * math.pi / NFFT)
    cosine = np.cos(steps).astype(np.float32).astype(ml_dtypes.bfloat16)
    sine = (-np.sin(steps)).astype(np.float32).astype(ml_dtypes.bfloat16)
    return np.concatenate([cosine[phase], sine[phase]], axis=0)


def whiten(spectra):
    lanes = spectra.shape[-1]
    values = spectra.astype(jnp.float32).reshape(spectra.shape[:2] + (3, 2) + spectra.shape[3:])
    square = values[:, :, :, 0] ** 2 + values[:, :, :, 1] ** 2
    band = np.arange(lanes) // BAND
    mean = jnp.asarray((band[:, None] == band[None, :]).astype(np.float32) / BAND)
    power = jnp.dot(square, mean, precision=lax.Precision.HIGHEST, preferred_element_type=jnp.float32)
    inverse = lax.rsqrt(power + 1e-06)
    return (values * inverse[:, :, :, None]).astype(jnp.bfloat16)


def pick(white, idx):
    hot = (idx[:, None] == jnp.arange(white.shape[1], dtype=jnp.int32)[None, :]).astype(jnp.bfloat16)
    flat = white.reshape(white.shape[0], white.shape[1], -1)
    hot = jnp.broadcast_to(hot[None], (white.shape[0],) + hot.shape)
    out = jnp.einsum("hps,hsx->hpx", hot, flat, preferred_element_type=jnp.float32)
    return out.astype(jnp.bfloat16).reshape(white.shape[0], idx.shape[0], 6, -1, 128)


def cross(own_rows, visit_rows):
    slots, tiles = (own_rows.shape[1], own_rows.shape[-2:])
    first, second = (own_rows.astype(jnp.float32), visit_rows.astype(jnp.float32))
    are, aim = (first[:, :, :, 0][:, :, :, None], first[:, :, :, 1][:, :, :, None])
    bre, bim = (second[:, :, :, 0][:, :, None], second[:, :, :, 1][:, :, None])
    real_part = jnp.sum(are * bre + aim * bim, axis=0).reshape((slots, 9) + tiles)
    imag_part = jnp.sum(are * bim - aim * bre, axis=0).reshape((slots, 9) + tiles)
    return jnp.concatenate([real_part, imag_part], axis=-2)


def sum_at_owner(value, axis, turn):
    count = lax.axis_size(axis)
    if count & (count - 1):
        return lax.psum_scatter(value, axis, scatter_dimension=0, tiled=True)
    owned, tail = value.shape[0] // count, value.shape[1:]
    bits = list(range(count.bit_length() - 1))
    others = bits[1:]
    if others:
        cut = turn % len(others)
        bits = bits[:1] + others[cut:] + others[:cut]
    me = lax.axis_index(axis)
    left = count.bit_length() - 1
    value = value.reshape((2,) * left + (owned,) + tail)
    for bit in bits:
        mine = lax.rem(lax.div(me, jnp.int32(1 << bit)), jnp.int32(2))
        dim = left - 1 - bit
        keep = lax.dynamic_slice_in_dim(value, mine, 1, dim)
        give = lax.dynamic_slice_in_dim(value, 1 - mine, 1, dim)
        swap = [(source, source ^ (1 << bit)) for source in range(count)]
        got = lax.ppermute(give.astype(jnp.bfloat16), axis, swap)
        value = keep.astype(jnp.float32) + got.astype(jnp.float32)
    return value.reshape((owned,) + tail)


def per_device(table, spectra, pairs, counts):
    n_tm = lax.axis_size("tm")
    n_sta = lax.axis_size("sta")
    hours_dev = spectra.shape[0]
    p_tile = pairs.shape[3]
    owned = p_tile // n_tm
    asked = [None] + [shifted(pairs[0, step, 1], "sta", -step) for step in range(1, n_sta)]
    own = [None] + [whiten(pick(spectra, pairs[0, step, 0])) for step in range(1, n_sta)]
    asked, own = lax.optimization_barrier((asked, own))
    picked = [pick(spectra, asked[step]) for step in range(1, n_sta)]
    home, *picked = lax.optimization_barrier((pairs[0, 0], *picked))
    own[0] = whiten(pick(spectra, home[0]))
    visits = [pick(spectra, home[1])] + [
        shifted(rows, "sta", step) for step, rows in enumerate(picked, 1)
    ]

    def reduce_tile(shift):
        limit = counts[0, shift]
        value = cross(own[shift], whiten(visits[shift]))
        slots = jnp.arange(p_tile, dtype=jnp.int32)
        value = jnp.where((slots < limit)[:, None, None, None], value, 0.0)
        return sum_at_owner(value.astype(jnp.bfloat16), "tm", shift)

    reduced = [reduce_tile(shift) for shift in range(n_sta)]
    rows = jnp.stack(reduced, axis=0).astype(jnp.bfloat16).reshape(n_sta * owned * 9, 2 * NF)
    lagged = jnp.dot(rows, table, preferred_element_type=jnp.float32)
    scale = 1.0 / math.sqrt(hours_dev * n_tm * NF)
    return (lagged * scale).astype(jnp.bfloat16).reshape(1, n_sta, owned, 9, LAGS)


def solution(mesh):
    mapped = jax.shard_map(
        per_device,
        mesh=mesh,
        in_specs=(
            P(None, None),
            P("tm", "sta", None, None),
            P("sta", None, None, None),
            P("sta", None),
        ),
        out_specs=P("sta", None, "tm", None, None),
        check_vma=False,
    )
    table = make_table()

    def run(spectra, pairs, counts):
        return mapped(jnp.asarray(table), spectra, pairs, counts)

    return run
```

```python
import math

import jax
import jax.numpy as jnp
import ml_dtypes
import numpy as np
from jax import lax
from jax.sharding import PartitionSpec as P

NF = 1024
NFFT = 8192
LAGS = 4001
BAND = 64


def shifted(value, axis, steps):
    count = lax.axis_size(axis)
    pairs = [(source, (source + steps) % count) for source in range(count)]
    return lax.ppermute(value, axis, pairs)


def make_table():
    freqs = np.arange(NF, dtype=np.int64)
    shifts = np.arange(LAGS, dtype=np.int64) - (LAGS - 1) // 2
    phase = np.mod(freqs[:, None] * shifts[None, :], NFFT)
    steps = np.arange(NFFT, dtype=np.float64) * (2.0 * math.pi / NFFT)
    cosine = np.cos(steps).astype(np.float32).astype(ml_dtypes.bfloat16)
    sine = (-np.sin(steps)).astype(np.float32).astype(ml_dtypes.bfloat16)
    return np.concatenate([cosine[phase], sine[phase]], axis=0)


def whiten(spectra):
    lanes = spectra.shape[-1]
    values = spectra.astype(jnp.float32).reshape(spectra.shape[:2] + (3, 2) + spectra.shape[3:])
    square = values[:, :, :, 0] ** 2 + values[:, :, :, 1] ** 2
    band = np.arange(lanes) // BAND
    mean = jnp.asarray((band[:, None] == band[None, :]).astype(np.float32) / BAND)
    power = jnp.dot(square, mean, precision=lax.Precision.HIGHEST, preferred_element_type=jnp.float32)
    inverse = lax.rsqrt(power + 1e-06)
    return (values * inverse[:, :, :, None]).astype(jnp.bfloat16)


def pick(white, idx):
    hot = (idx[:, None] == jnp.arange(white.shape[1], dtype=jnp.int32)[None, :]).astype(jnp.bfloat16)
    flat = white.reshape(white.shape[0], white.shape[1], -1)
    hot = jnp.broadcast_to(hot[None], (white.shape[0],) + hot.shape)
    out = jnp.einsum("hps,hsx->hpx", hot, flat, preferred_element_type=jnp.float32)
    return out.astype(jnp.bfloat16).reshape(white.shape[0], idx.shape[0], 6, -1, 128)


def cross(own_rows, visit_rows):
    slots, tiles = (own_rows.shape[1], own_rows.shape[-2:])
    first, second = (own_rows.astype(jnp.float32), visit_rows.astype(jnp.float32))
    are, aim = (first[:, :, :, 0][:, :, :, None], first[:, :, :, 1][:, :, :, None])
    bre, bim = (second[:, :, :, 0][:, :, None], second[:, :, :, 1][:, :, None])
    real_part = jnp.sum(are * bre + aim * bim, axis=0).reshape((slots, 9) + tiles)
    imag_part = jnp.sum(are * bim - aim * bre, axis=0).reshape((slots, 9) + tiles)
    return jnp.concatenate([real_part, imag_part], axis=-2)


def sum_at_owner(value, axis, turn):
    count = lax.axis_size(axis)
    if count & (count - 1):
        return lax.psum_scatter(value, axis, scatter_dimension=0, tiled=True)
    owned, tail = value.shape[0] // count, value.shape[1:]
    bits = list(range(count.bit_length() - 1))
    others = bits[1:]
    if others:
        cut = turn % len(others)
        bits = bits[:1] + others[cut:] + others[:cut]
    me = lax.axis_index(axis)
    left = count.bit_length() - 1
    value = value.reshape((2,) * left + (owned,) + tail)
    for bit in bits:
        mine = lax.rem(lax.div(me, jnp.int32(1 << bit)), jnp.int32(2))
        dim = left - 1 - bit
        keep = lax.dynamic_slice_in_dim(value, mine, 1, dim)
        give = lax.dynamic_slice_in_dim(value, 1 - mine, 1, dim)
        swap = [(source, source ^ (1 << bit)) for source in range(count)]
        got = lax.ppermute(give.astype(jnp.bfloat16), axis, swap)
        value = keep.astype(jnp.float32) + got.astype(jnp.float32)
    return value.reshape((owned,) + tail)


def per_device(table, spectra, pairs, counts):
    n_tm = lax.axis_size("tm")
    n_sta = lax.axis_size("sta")
    hours_dev = spectra.shape[0]
    p_tile = pairs.shape[3]
    owned = p_tile // n_tm
    asked = [None] + [shifted(pairs[0, step, 1], "sta", -step) for step in range(1, n_sta)]
    own = [None] + [whiten(pick(spectra, pairs[0, step, 0])) for step in range(1, n_sta)]
    asked, own = lax.optimization_barrier((asked, own))
    picked = [pick(spectra, asked[step]) for step in range(1, n_sta)]
    home, *picked = lax.optimization_barrier((pairs[0, 0], *picked))
    own[0] = whiten(pick(spectra, home[0]))
    visits = [pick(spectra, home[1])] + [
        shifted(rows, "sta", step) for step, rows in enumerate(picked, 1)
    ]

    def reduce_tile(shift):
        limit = counts[0, shift]
        value = cross(own[shift], whiten(visits[shift]))
        slots = jnp.arange(p_tile, dtype=jnp.int32)
        value = jnp.where((slots < limit)[:, None, None, None], value, 0.0)
        return sum_at_owner(value.astype(jnp.bfloat16), "tm", shift)

    early = sorted({0, n_sta - 1})
    reduced = {shift: reduce_tile(shift) for shift in early}
    late = [shift for shift in range(n_sta) if shift not in early]
    reduced, arrived = lax.optimization_barrier((reduced, [visits[shift] for shift in late]))
    for shift, rows in zip(late, arrived):
        visits[shift] = rows
        reduced[shift] = reduce_tile(shift)
    reduced = [reduced[shift] for shift in range(n_sta)]
    rows = jnp.stack(reduced, axis=0).astype(jnp.bfloat16).reshape(n_sta * owned * 9, 2 * NF)
    lagged = jnp.dot(rows, table, preferred_element_type=jnp.float32)
    scale = 1.0 / math.sqrt(hours_dev * n_tm * NF)
    return (lagged * scale).astype(jnp.bfloat16).reshape(1, n_sta, owned, 9, LAGS)


def solution(mesh):
    mapped = jax.shard_map(
        per_device,
        mesh=mesh,
        in_specs=(
            P(None, None),
            P("tm", "sta", None, None),
            P("sta", None, None, None),
            P("sta", None),
        ),
        out_specs=P("sta", None, "tm", None, None),
        check_vma=False,
    )
    table = make_table()

    def run(spectra, pairs, counts):
        return mapped(jnp.asarray(table), spectra, pairs, counts)

    return run
```

```python
import math

import jax
import jax.numpy as jnp
import ml_dtypes
import numpy as np
from jax import lax
from jax.sharding import PartitionSpec as P

NF = 1024
NFFT = 8192
LAGS = 4001
BAND = 64


def shifted(value, axis, steps):
    count = lax.axis_size(axis)
    pairs = [(source, (source + steps) % count) for source in range(count)]
    return lax.ppermute(value, axis, pairs)


def make_table():
    freqs = np.arange(NF, dtype=np.int64)
    shifts = np.arange(LAGS, dtype=np.int64) - (LAGS - 1) // 2
    phase = np.mod(freqs[:, None] * shifts[None, :], NFFT)
    steps = np.arange(NFFT, dtype=np.float64) * (2.0 * math.pi / NFFT)
    cosine = np.cos(steps).astype(np.float32).astype(ml_dtypes.bfloat16)
    sine = (-np.sin(steps)).astype(np.float32).astype(ml_dtypes.bfloat16)
    return np.concatenate([cosine[phase], sine[phase]], axis=0)


def whiten(spectra):
    lanes = spectra.shape[-1]
    values = spectra.astype(jnp.float32).reshape(spectra.shape[:2] + (3, 2) + spectra.shape[3:])
    square = values[:, :, :, 0] ** 2 + values[:, :, :, 1] ** 2
    band = np.arange(lanes) // BAND
    mean = jnp.asarray((band[:, None] == band[None, :]).astype(np.float32) / BAND)
    power = jnp.dot(square, mean, precision=lax.Precision.HIGHEST, preferred_element_type=jnp.float32)
    inverse = lax.rsqrt(power + 1e-06)
    return (values * inverse[:, :, :, None]).astype(jnp.bfloat16)


def pick(white, idx, limit=None):
    hot = (idx[:, None] == jnp.arange(white.shape[1], dtype=jnp.int32)[None, :]).astype(jnp.bfloat16)
    if limit is not None:
        hot = hot * (jnp.arange(idx.shape[0], dtype=jnp.int32) < limit).astype(hot.dtype)[:, None]
    flat = white.reshape(white.shape[0], white.shape[1], -1)
    hot = jnp.broadcast_to(hot[None], (white.shape[0],) + hot.shape)
    out = jnp.einsum("hps,hsx->hpx", hot, flat, preferred_element_type=jnp.float32)
    return out.astype(jnp.bfloat16).reshape(white.shape[0], idx.shape[0], 6, -1, 128)


def cross(own_rows, visit_rows):
    slots, tiles = (own_rows.shape[1], own_rows.shape[-2:])
    first, second = (own_rows.astype(jnp.float32), visit_rows.astype(jnp.float32))
    are, aim = (first[:, :, :, 0][:, :, :, None], first[:, :, :, 1][:, :, :, None])
    bre, bim = (second[:, :, :, 0][:, :, None], second[:, :, :, 1][:, :, None])
    real_part = jnp.sum(are * bre + aim * bim, axis=0).reshape((slots, 9) + tiles)
    imag_part = jnp.sum(are * bim - aim * bre, axis=0).reshape((slots, 9) + tiles)
    return jnp.concatenate([real_part, imag_part], axis=-2)


def sum_at_owner(value, axis, turn):
    count = lax.axis_size(axis)
    if count & (count - 1):
        return lax.psum_scatter(value, axis, scatter_dimension=0, tiled=True)
    owned, tail = value.shape[0] // count, value.shape[1:]
    bits = list(range(count.bit_length() - 1))
    others = bits[1:]
    if others:
        cut = turn % len(others)
        bits = bits[:1] + others[cut:] + others[:cut]
    me = lax.axis_index(axis)
    left = count.bit_length() - 1
    value = value.reshape((2,) * left + (owned,) + tail)
    for bit in bits:
        mine = lax.rem(lax.div(me, jnp.int32(1 << bit)), jnp.int32(2))
        dim = left - 1 - bit
        keep = lax.dynamic_slice_in_dim(value, mine, 1, dim)
        give = lax.dynamic_slice_in_dim(value, 1 - mine, 1, dim)
        swap = [(source, source ^ (1 << bit)) for source in range(count)]
        got = lax.ppermute(give.astype(jnp.bfloat16), axis, swap)
        value = keep.astype(jnp.float32) + got.astype(jnp.float32)
    return value.reshape((owned,) + tail)


def per_device(table, spectra, pairs, counts):
    n_tm = lax.axis_size("tm")
    n_sta = lax.axis_size("sta")
    hours_dev = spectra.shape[0]
    owned = pairs.shape[3] // n_tm
    asked = [None] + [shifted(pairs[0, step, 1], "sta", -step) for step in range(1, n_sta)]
    own = [None] + [whiten(pick(spectra, pairs[0, step, 0], counts[0, step])) for step in range(1, n_sta)]
    asked, own = lax.optimization_barrier((asked, own))
    picked = [pick(spectra, asked[step]) for step in range(1, n_sta)]
    visits = [None] + [shifted(rows, "sta", step) for step, rows in enumerate(picked, 1)]
    home, visits[-1] = lax.optimization_barrier((pairs[0, 0], visits[-1]))
    own[0] = whiten(pick(spectra, home[0], counts[0, 0]))
    visits[0] = pick(spectra, home[1])

    def reduce_tile(shift):
        value = cross(own[shift], whiten(visits[shift]))
        return sum_at_owner(value.astype(jnp.bfloat16), "tm", shift)

    early = sorted({0, n_sta - 1})
    reduced = {shift: reduce_tile(shift) for shift in early}
    late = [shift for shift in range(n_sta) if shift not in early]
    reduced, arrived = lax.optimization_barrier((reduced, [visits[shift] for shift in late]))
    for shift, rows in zip(late, arrived):
        visits[shift] = rows
        reduced[shift] = reduce_tile(shift)
    reduced = [reduced[shift] for shift in range(n_sta)]
    rows = jnp.stack(reduced, axis=0).astype(jnp.bfloat16).reshape(n_sta * owned * 9, 2 * NF)
    lagged = jnp.dot(rows, table, preferred_element_type=jnp.float32)
    scale = 1.0 / math.sqrt(hours_dev * n_tm * NF)
    return (lagged * scale).astype(jnp.bfloat16).reshape(1, n_sta, owned, 9, LAGS)


def solution(mesh):
    mapped = jax.shard_map(
        per_device,
        mesh=mesh,
        in_specs=(
            P(None, None),
            P("tm", "sta", None, None),
            P("sta", None, None, None),
            P("sta", None),
        ),
        out_specs=P("sta", None, "tm", None, None),
        check_vma=False,
    )
    table = make_table()

    def run(spectra, pairs, counts):
        return mapped(jnp.asarray(table), spectra, pairs, counts)

    return run
```
